32 devices in a mesh: ka: 4 (over z), row: 2 (over x), col: 4 (over y, core).
Axes of the slice: x: 2, y: 2, z: 4, core: 2. Of those that a mesh axis runs over, the one named last changes fastest.
Arguments:
- screened_q: bfloat16 [2, 64, 2, 32, 20480], P(None, ('ka', 'row'), None, None, 'col'), may hold values from -48 to 48
- three_centre: bfloat16 [20480, 7168], P('col', 'row'), may hold values from -0.0390625 to 0.0390625
- green_fn: bfloat16 [2, 64, 112, 7168], P(None, 'ka', None, ('row', 'col')), may hold values from -0.0625 to 0.0625
- mask_three: int32 [128, 128], P('col', 'row'), may hold values 0 or 1
- mask_green: int32 [64, 2, 128], P('ka', None, ('row', 'col')), may hold values 0 or 1
- cell_list: int32 [64], replicated, may hold values from 0 to 63, each once
Outputs:
- sigma_window: float32 [2, 64, 32, 112], P(None, 'ka')
The draws below stay inside these ranges and needn't reach their ends.
Inputs may be any that keep to these rules, and one draw needn't show every extreme that they name: `cell_list`: each of the 64 cell numbers appears once.
All inputs are finite; a program needn't handle non-finite values. No bound on the sum of `mask_three` or of `mask_green` on one device may be relied on, other than what follows from the above.
Results may differ from the reference program's by a relative error of at most 0.0041.
Values may be sent and summed in bfloat16 or wider, within the bound.
A program may use at most 192 MiB of HBM per device.

```python
import math
import jax
import jax.numpy as jnp
from jax import lax

KA = 8
KB = 8
NQ = 64
TAU = 2
PS = 32
NAUX = 20480
NORB = 7168
NAB = 128
NOB = 128
OWB = 2
OS = 112


def place_ends(entries, key, low, high):
    longest = entries.shape.index(max(entries.shape))
    spots = []
    for shift in (0, 1):
        where = [jax.random.randint(jax.random.fold_in(key, axis), (), 0, length) for axis, length in enumerate(entries.shape)]
        where[longest] = (where[longest] + shift) % entries.shape[longest]
        spots.append(tuple(where))
    return entries.at[spots[0]].set(low).at[spots[1]].set(high)


def levels(own_key, extent, cuts, smallest, high):
    gain, own = 1.0, jax.random.fold_in(own_key, 6)
    for position, parts in cuts:
        steps = jnp.exp(jax.random.uniform(jax.random.fold_in(own, position), (parts,), jnp.float32, smallest / len(cuts), high / len(cuts)))
        gain = gain * jnp.repeat(steps, extent[position] // parts).reshape([-1 if axis == position else 1 for axis in range(len(extent))])
    return gain


def normal_values(key, extent, scale, bound, cuts=(), held_as=jnp.bfloat16):
    array = scale * jax.random.normal(key, extent, jnp.float32)
    if cuts:
        array = array * levels(key, extent, cuts, -0.22, 0.18)
    return jnp.clip(array, -bound, bound).astype(held_as)


def setup_inputs(seed: int = 0) -> dict:
    key_of = jax.random.split(jax.random.key(seed), 7)
    return {
        "screened_q": normal_values(key_of[0], (TAU, NQ, 2, PS, NAUX), 8.0, 48.0, ((1, 8), (4, 4))),
        "three_centre": normal_values(key_of[1], (NAUX, NORB), NAUX ** -0.5, 0.0390625, ((0, 4), (1, 2))),
        "green_fn": normal_values(key_of[2], (TAU, NQ, OS, NORB), NORB ** -0.5, 0.0625, ((1, 4), (3, 8))),
        "mask_three": place_ends((jax.random.randint(key_of[3], (NAB, NOB), 0, 4) < 3).astype(jnp.int32), jax.random.fold_in(key_of[3], 1), 0, 1),
        "mask_green": place_ends((jax.random.randint(key_of[4], (NQ, OWB, NOB), 0, 4) < 3).astype(jnp.int32), jax.random.fold_in(key_of[4], 1), 0, 1),
        "cell_list": jax.random.permutation(key_of[5], NQ).astype(jnp.int32),
    }


def phase_table(cell_list, q_order):
    q_count = KA * KB
    q_first = q_order // KB
    q_second = q_order % KB
    cell_first = cell_list // KB
    cell_second = cell_list % KB
    phase_turns = (cell_first[:, None] * q_first[None, :] * KB + cell_second[:, None] * q_second[None, :] * KA) % q_count
    angles = phase_turns.astype(jnp.float32) * (2.0 * math.pi / q_count)
    return (jnp.stack([jnp.cos(angles), -jnp.sin(angles)], axis=2) / q_count).astype(jnp.bfloat16)


def reference(screened_q, three_centre, green_fn, mask_three, mask_green, cell_list):
    phases = phase_table(cell_list, jnp.arange(NQ, dtype=jnp.int32))
    screened_cell = jnp.einsum("rqc,tqcpa->trpa", phases.astype(jnp.float32), screened_q.astype(jnp.float32), precision=lax.Precision.HIGHEST).astype(jnp.bfloat16)
    keep_three = jnp.repeat(jnp.repeat(mask_three.astype(jnp.bfloat16), NAUX // NAB, axis=0), NORB // NOB, axis=1)
    three_masked = three_centre * keep_three
    mixed = jnp.dot(screened_cell.reshape(TAU * NQ * PS, NAUX), three_masked, preferred_element_type=jnp.float32)
    mixed = mixed.astype(jnp.bfloat16).reshape(TAU, NQ, PS, NORB)
    keep_green = jnp.repeat(jnp.repeat(mask_green.astype(jnp.bfloat16), NORB // NOB, axis=1), NORB // NOB, axis=2)
    green_masked = green_fn * keep_green[None]

    def per_time(pair_in):
        mix_part, green_part = pair_in
        return jnp.einsum("rpn,rmn->rpm", mix_part.astype(jnp.float32), green_part.astype(jnp.float32))

    return lax.map(per_time, (mixed, green_masked))
```

```python
import functools
import math

import jax
import jax.numpy as jnp
from jax import lax
from jax.experimental import pallas as pl
from jax.experimental.pallas import tpu as pltpu
from jax.sharding import PartitionSpec as P

KA = 8
KB = 8
P_PARTS = 2
LANES = 256
GREEN_CELLS = 4
VMEM_BYTES = 63 * 1024 * 1024


def phase_table(cell_list, q_order):
    q_count = KA * KB
    q_first = q_order // KB
    q_second = q_order % KB
    cell_first = cell_list // KB
    cell_second = cell_list % KB
    phase_turns = (
        cell_first[:, None] * q_first[None, :] * KB + cell_second[:, None] * q_second[None, :] * KA
    ) % q_count
    angles = phase_turns.astype(jnp.float32) * (2.0 * math.pi / q_count)
    return (jnp.stack([jnp.cos(angles), -jnp.sin(angles)], axis=2) / q_count).astype(jnp.bfloat16)


def two_terms(value):
    high = value.astype(jnp.bfloat16)
    return high, (value - high.astype(jnp.float32)).astype(jnp.bfloat16)


def remote(src, dst, send_sem, recv_sem, device_id):
    return pltpu.make_async_remote_copy(
        src_ref=src,
        dst_ref=dst,
        send_sem=send_sem,
        recv_sem=recv_sem,
        device_id=device_id,
        device_id_type=pl.DeviceIdType.MESH,
    )


def kernel(
    counts, share, by_part,
    x_ref, three_ref, green_ref, keep_three_ref, keep_green_ref, phase_ref,
    out_ref, land_ref,
    three, x_rows, parts, got_core, z_rows, send_y, got_y, send_z, got_z, own_z,
    green, sigma, got_sum, total, gathered,
    three_sem, row_sem, green_sem, x_send, x_recv, core_send, core_recv, y_send, y_recv,
    z_send, z_recv, sum_send, sum_recv, all_send, all_recv,
):
    ka_count, row_count, col_count = counts
    tau_count, q_local, planes, slab_rows, aux_local = x_ref.shape
    chunks, p_part = land_ref.shape[0], land_ref.shape[4]
    halves = chunks // tau_count
    rows = q_local * planes * p_part
    cells = keep_green_ref.shape[0]
    cell_groups = cells // GREEN_CELLS
    cell_rows = cells * p_part
    aux_blocks = keep_three_ref.shape[1]
    block = aux_local // aux_blocks
    n_part = three.shape[2]
    group = row_count * col_count
    ka, row, col = lax.axis_index("ka"), lax.axis_index("row"), lax.axis_index("col")
    place = row * col_count + col
    low_bit, high_bit = col % 2, col // 2
    core_peer = {"col": col + 1 - 2 * low_bit}
    y_peer = {"col": (col + 2) % 4}

    def member(step):
        other = (place + step) % group
        return other, {"row": other // col_count, "col": other % col_count}

    def three_copy(c):
        source = three_ref.at[c] if by_part else three_ref.at[:, pl.ds(c * n_part, n_part)]
        return pltpu.make_async_copy(source, three.at[c], three_sem.at[c])

    def green_copy(number):
        source = green_ref.at[
            number // (halves * cell_groups), pl.ds((number % cell_groups) * GREEN_CELLS, GREEN_CELLS)
        ]
        return pltpu.make_async_copy(source, green.at[number % 2], green_sem.at[number % 2])

    def own_rows(k):
        return x_ref.at[k // halves, :, :, pl.ds((k % halves) * p_part, p_part), :]

    def x_copy(k, s):
        return remote(
            own_rows(k), land_ref.at[k, s - 1], x_send.at[k, s - 1], x_recv.at[k, s - 1],
            {"row": (row + row_count - s) % row_count},
        )

    def core_copy(slot, j):
        return remote(
            parts.at[j], got_core.at[slot, j], core_send.at[j], core_recv.at[slot, j], core_peer
        )

    def y_copy(slot, s):
        return remote(send_y, got_y.at[slot, s], y_send, y_recv.at[slot, s], y_peer)

    def z_copy(slot, s):
        return remote(
            send_z.at[s - 1], got_z.at[slot, s - 1], z_send.at[s - 1], z_recv.at[slot, s - 1],
            {"ka": (ka + s) % ka_count},
        )

    for c in range(col_count):
        three_copy(c).start()
    for number in range(2):
        green_copy(number).start()

    barrier = pltpu.get_barrier_semaphore()
    for step in range(1, group):
        pl.semaphore_signal(
            barrier, inc=1, device_id=member(step)[1], device_id_type=pl.DeviceIdType.MESH
        )
    for step in range(1, ka_count):
        pl.semaphore_signal(
            barrier, inc=1, device_id={"ka": (ka + step) % ka_count},
            device_id_type=pl.DeviceIdType.MESH,
        )
    pl.semaphore_wait(barrier, group - 1 + ka_count - 1)

    for k in range(min(2, chunks)):
        for s in range(1, row_count):
            x_copy(k, s).start()

    for c in range(col_count):
        three_copy(c).wait()

    def mask_block(i, carry):
        c, b = i // aux_blocks, i % aux_blocks
        keep = keep_three_ref[c, pl.ds(b, 1), :].astype(jnp.bfloat16)
        here = pl.ds(pl.multiple_of(b * block, 16), block)
        three[c, here, :] = three[c, here, :] * keep
        return carry

    lax.fori_loop(0, col_count * aux_blocks, mask_block, 0)

    def unit(k, s):
        number = k * row_count + s
        slot = number % 2
        here = pl.ds(pl.multiple_of(s * rows, 8), rows)

        def multiply(o, carry):
            c = jnp.where(
                o < 2,
                2 * o + 1 - low_bit,
                2 * jnp.where(o == 2, 1 - high_bit, high_bit) + low_bit,
            )
            for first in range(0, n_part, LANES):
                lanes = slice(first, min(first + LANES, n_part))
                value = jnp.dot(
                    x_rows[...].reshape(rows, aux_local),
                    three[c, :, lanes],
                    preferred_element_type=jnp.float32,
                )

                @pl.when(o < 3)
                def _():
                    parts[jnp.minimum(o, 2), :, lanes] = value

                @pl.when(o == 3)
                def _():
                    z_rows[here, lanes] = value

            @pl.when(o < 2)
            def _():
                core_copy(slot, o).start()

            return carry

        lax.fori_loop(0, 4, multiply, 0)
        for j in range(2):
            core_copy(slot, j).wait_recv()

        @pl.when(number > 0)
        def _():
            y_copy(0, 0).wait_send()

        send_y[...] = (parts[2] + got_core[slot, 1 - high_bit]).astype(jnp.bfloat16)
        y_copy(k % 2, s).start()
        z_rows[here, :] += got_core[slot, high_bit]
        for j in range(2):
            core_copy(slot, j).wait_send()

    def finish(k):
        for s in range(1, ka_count):
            z_copy(k % 2, s).wait()

        def cell(r, carry):
            number = k * cell_groups + r // GREEN_CELLS

            @pl.when(r % GREEN_CELLS == 0)
            def _():
                green_copy(number).wait()

            here = pl.ds(pl.multiple_of(r * p_part, 16), p_part)
            mixed = own_z[here, :]
            for s in range(ka_count - 1):
                mixed = mixed + got_z[k % 2, s, here, :].astype(jnp.float32)
            lines = []
            for o in range(keep_green_ref.shape[1]):
                lines.extend(two_terms(mixed * keep_green_ref[r, o : o + 1, :]))
            both = lax.dot_general(
                jnp.concatenate(lines, axis=0),
                green[number % 2, r % GREEN_CELLS],
                (((1,), (1,)), ((), ())),
                preferred_element_type=jnp.float32,
            )
            width = both.shape[1] // keep_green_ref.shape[1]
            lane = lax.broadcasted_iota(jnp.int32, (p_part, both.shape[1]), 1) // width
            value = jnp.zeros((p_part, both.shape[1]), jnp.float32)
            for o in range(keep_green_ref.shape[1]):
                first = 2 * o * p_part
                summed = both[first : first + p_part] + both[first + p_part : first + 2 * p_part]
                value = jnp.where(lane == o, summed, value)
            sigma[pl.ds(pl.multiple_of(k * cell_rows + r * p_part, 8), p_part), :] = value

            @pl.when(
                jnp.logical_and(
                    r % GREEN_CELLS == GREEN_CELLS - 1, number + 2 < chunks * cell_groups
                )
            )
            def _():
                green_copy(number + 2).start()

            return carry

        lax.fori_loop(0, cells, cell, 0)

    def chunk(k, carry):
        load = pltpu.make_async_copy(own_rows(k), x_rows, row_sem)
        load.start()
        load.wait()
        unit(k, 0)

        @pl.when(k > 0)
        def _():
            finish(k - 1)

        def other_row(s, carry):
            x_copy(k, s).wait()

            @pl.when(k + 2 < chunks)
            def _():
                x_copy(k + 2, s).start()

            load = pltpu.make_async_copy(land_ref.at[k, s - 1], x_rows, row_sem)
            load.start()
            load.wait()
            unit(k, s)
            return carry

        lax.fori_loop(1, row_count, other_row, 0)

        for s in range(row_count):
            y_copy(k % 2, s).wait_recv()
            z_rows[s * rows : (s + 1) * rows, :] += got_y[k % 2, s].astype(jnp.float32)

        for first in range(0, n_part, LANES):
            lanes = slice(first, min(first + LANES, n_part))
            high, low = two_terms(z_rows[:, lanes])
            for s in range(ka_count):
                phases = phase_ref[s * cell_rows : (s + 1) * cell_rows, :]
                part = jnp.dot(phases, high, preferred_element_type=jnp.float32)
                part = part + jnp.dot(phases, low, preferred_element_type=jnp.float32)
                if s == 0:
                    own_z[:, lanes] = part
                else:
                    send_z[s - 1, :, lanes] = part.astype(jnp.bfloat16)
        for s in range(1, ka_count):
            z_copy(k % 2, s).start()
        return carry

    lax.fori_loop(0, chunks, chunk, 0)
    y_copy(0, 0).wait_send()
    finish(chunks - 1)

    if share == 0:
        out_ref[...] = sigma[...]
        return

    def sum_copy(step):
        other, device_id = member(step)
        return remote(
            sigma.at[pl.ds(pl.multiple_of(other * share, 8), share)], got_sum.at[step - 1],
            sum_send.at[step - 1], sum_recv.at[step - 1], device_id,
        )

    mine = pl.ds(pl.multiple_of(place * share, 8), share)

    def all_copy(step):
        return remote(
            total, gathered.at[mine], all_send.at[step - 1], all_recv.at[step - 1], member(step)[1]
        )

    for step in range(1, group):
        sum_copy(step).start()
    value = sigma[mine, :]
    for step in range(1, group):
        sum_copy(step).wait_recv()
        value = value + got_sum[step - 1]
    total[...] = value
    for step in range(1, group):
        all_copy(step).start()
    gathered[mine, :] = value
    for step in range(1, group):
        sum_copy(step).wait_send()
        all_copy(step).wait()
    out_ref[...] = gathered[...]


def on_device(screened_q, three_centre, green_fn, mask_three, mask_green, cell_list):
    counts = tuple(lax.axis_size(name) for name in ("ka", "row", "col"))
    ka_count, row_count, col_count = counts
    ka, row = lax.axis_index("ka"), lax.axis_index("row")
    tau_count, q_local, planes, slab_rows, aux_local = screened_q.shape
    orb_cols = three_centre.shape[1]
    n_part = orb_cols // col_count
    q_total = KA * KB
    cells = q_total // ka_count
    p_part = slab_rows // P_PARTS
    chunks = tau_count * P_PARTS
    rows = q_local * planes * p_part
    cell_rows = cells * p_part
    window = green_fn.shape[2]

    table = phase_table(jnp.roll(cell_list, -ka * cells), jnp.arange(q_total, dtype=jnp.int32))
    columns = [
        lax.dynamic_slice_in_dim(
            table, (ka * row_count + (row + s) % row_count) * q_local, q_local, axis=1
        )
        for s in range(row_count)
    ]
    phases = jnp.concatenate(columns, axis=1).reshape(q_total, row_count * q_local * planes)
    same = jnp.eye(p_part, dtype=jnp.bfloat16)
    phases = (phases[:, None, :, None] * same[None, :, None, :]).reshape(
        q_total * p_part, row_count * rows
    )

    keep_three = jnp.repeat(mask_three.astype(jnp.float32), orb_cols // mask_three.shape[1], axis=1)
    keep_three = keep_three.reshape(-1, col_count, n_part).transpose(1, 0, 2)
    keep_green = jnp.repeat(
        mask_green.astype(jnp.float32), green_fn.shape[3] // mask_green.shape[2], axis=2
    )
    by_part = n_part % 128 != 0
    if by_part:
        three_centre = three_centre.reshape(aux_local, col_count, n_part).transpose(1, 0, 2)

    group = row_count * col_count
    sigma_rows = chunks * cell_rows
    share = sigma_rows // group if sigma_rows % (8 * group) == 0 else 0
    any_space = pl.BlockSpec(memory_space=pl.ANY)
    vmem = pl.BlockSpec(memory_space=pltpu.VMEM)
    f32, bf16 = jnp.float32, jnp.bfloat16
    dma = pltpu.SemaphoreType.DMA
    sigma, _ = pl.pallas_call(
        functools.partial(kernel, counts, share, by_part),
        out_shape=(
            jax.ShapeDtypeStruct((sigma_rows, window), f32),
            jax.ShapeDtypeStruct(
                (chunks, row_count - 1, q_local, planes, p_part, aux_local), bf16
            ),
        ),
        in_specs=[any_space] * 3 + [vmem] * 3,
        out_specs=(vmem, any_space),
        scratch_shapes=[
            pltpu.VMEM((col_count, aux_local, n_part), bf16),
            pltpu.VMEM((q_local, planes, p_part, aux_local), bf16),
            pltpu.VMEM((3, rows, n_part), f32),
            pltpu.VMEM((2, 2, rows, n_part), f32),
            pltpu.VMEM((row_count * rows, n_part), f32),
            pltpu.VMEM((rows, n_part), bf16),
            pltpu.VMEM((2, row_count, rows, n_part), bf16),
            pltpu.VMEM((ka_count - 1, cell_rows, n_part), bf16),
            pltpu.VMEM((2, ka_count - 1, cell_rows, n_part), bf16),
            pltpu.VMEM((cell_rows, n_part), f32),
            pltpu.VMEM((2, GREEN_CELLS, window, n_part), bf16),
            pltpu.VMEM((sigma_rows, window), f32),
            pltpu.VMEM((group - 1, max(share, 8), window), f32),
            pltpu.VMEM((max(share, 8), window), f32),
            pltpu.VMEM((sigma_rows, window), f32),
            dma((col_count,)),
            dma,
            dma((2,)),
            dma((chunks, row_count - 1)),
            dma((chunks, row_count - 1)),
            dma((2,)),
            dma((2, 2)),
            dma,
            dma((2, row_count)),
            dma((ka_count - 1,)),
            dma((2, ka_count - 1)),
            dma((group - 1,)),
            dma((group - 1,)),
            dma((group - 1,)),
            dma((group - 1,)),
        ],
        compiler_params=pltpu.CompilerParams(
            collective_id=0, has_side_effects=True, vmem_limit_bytes=VMEM_BYTES
        ),
    )(screened_q, three_centre, green_fn, keep_three, keep_green, phases)
    sigma = sigma.reshape(tau_count, P_PARTS, cells, p_part, window)
    sigma = sigma.transpose(0, 2, 1, 3, 4).reshape(tau_count, cells, slab_rows, window)
    return sigma if share else lax.psum(sigma, ("row", "col"))


def solution(mesh):
    return jax.shard_map(
        on_device,
        mesh=mesh,
        in_specs=(
            P(None, ("ka", "row"), None, None, "col"),
            P("col", "row"),
            P(None, "ka", None, ("row", "col")),
            P("col", "row"),
            P("ka", None, ("row", "col")),
            P(),
        ),
        out_specs=P(None, "ka", None, None),
        check_vma=False,
    )
```
